256 devices in a mesh: cells: 8 (over x, core), genes: 32 (over z, y).
Axes of the slice: x: 4, y: 4, z: 8, core: 2. Of those that a mesh axis runs over, the one named last changes fastest.
Arguments:
- expression: bfloat16 [16384, 61440], P('cells', 'genes'), may hold values from -6 to 6
- labels: int32 [16384], P('cells'), may hold values from 0 to 255, as said below
Outputs:
- welch_t: float32 [256, 61440], P(('cells', 'genes'))
- fold_change: float32 [256, 61440], P(('cells', 'genes'))
The draws below stay inside these ranges and needn't reach their ends.
Inputs may be any that keep to these rules, and one draw needn't show every extreme that they name: `labels`: every cluster holds at least two cells.
All inputs are finite; a program needn't handle non-finite values.
Results may differ from the reference program's by a relative error of at most 0.0003.
Values sent between devices are 32-bit elements; how exact they have to be, the bound alone decides.
A program may use at most 64 MiB of HBM per device.

```python
import jax
import jax.numpy as jnp
from jax import lax

G = 61440
K = 256
CELL_DEV = 2048
CELLS = 16384
N_CELLS = 8
N_GENES = 32


def draw_labels(key, part):
    key = jax.random.fold_in(key, 11)
    first, second, third, fourth = jax.random.split(key, 4)
    total = CELL_DEV * N_CELLS
    position = jnp.arange(total, dtype=jnp.int32)
    slab = position // CELL_DEV
    pick = jax.random.randint(first, (total,), 0, 4 * (N_CELLS - 1))
    even_side = pick < N_CELLS - 1 + 2 * slab
    left = jax.random.randint(second, (total,), 0, K // 2)
    right = jax.random.randint(third, (total,), 0, K // 2)
    halfway = left * right // (K // 2)
    labels = 2 * halfway + jnp.where(even_side, 0, 1).astype(jnp.int32)
    pairs = jnp.repeat(jax.random.permutation(fourth, K).astype(jnp.int32), 2)
    return jnp.concatenate([pairs, labels[2 * K:]]).astype(jnp.int32)


def block_levels(own_key, extent, cuts, smallest, top_value):
    loudness = 1.0
    for dim, blocks in cuts:
        draws = jax.random.uniform(jax.random.fold_in(jax.random.fold_in(own_key, 6), dim), (blocks,), jnp.float32, smallest / len(cuts), top_value / len(cuts))
        loudness = loudness * jnp.repeat(jnp.exp(draws), extent[dim] // blocks).reshape((-1,) + (1,) * (len(extent) - 1 - dim))
    return loudness


def scatter_about(stream_key, dims, deviation, reach, cuts=(), held_as=jnp.bfloat16):
    entries = deviation * jax.random.normal(stream_key, dims, jnp.float32)
    if cuts:
        entries = entries * block_levels(stream_key, dims, cuts, -0.22, 0.18)
    return jnp.clip(entries, -reach, reach).astype(held_as)


def setup_inputs(seed: int = 0) -> dict:
    seeds = jax.random.split(jax.random.key(seed), 3)
    return {
        "expression": scatter_about(seeds[0], (CELLS, G), 1.0, 6.0, ((0, 8), (1, 32))),
        "labels": draw_labels(jax.random.fold_in(seeds[2], 71), 0),
    }


def welch(sums, squares, sizes, total_sum, total_squares, cells_all):
    mean_in = sums / sizes
    var_in = jnp.maximum((squares - sums * mean_in) / (sizes - 1.0), 0.1)
    rest = cells_all - sizes
    rest_sum = total_sum - sums
    mean_out = rest_sum / rest
    var_out = jnp.maximum((total_squares - squares - rest_sum * mean_out) / (rest - 1.0), 0.1)
    fold = mean_in - mean_out
    return (fold / jnp.sqrt(var_in / sizes + var_out / rest), fold)

def reference(expression, labels):
    cells_all = expression.shape[0]
    blocks = G // N_GENES
    sizes = jax.ops.segment_sum(jnp.ones((cells_all,), jnp.float32), labels, K)[:, None]

    def one_block(index):
        start = (index * blocks).astype(jnp.int32)
        piece = lax.dynamic_slice_in_dim(expression, start, blocks, 1).astype(jnp.float32)
        squared = piece * piece
        sums = jax.ops.segment_sum(piece, labels, K)
        squares = jax.ops.segment_sum(squared, labels, K)
        total_sum = lax.optimization_barrier(jnp.sum(sums, axis=0, keepdims=True))
        total_squares = lax.optimization_barrier(jnp.sum(squares, axis=0, keepdims=True))
        return welch(sums, squares, sizes, total_sum, total_squares, jnp.float32(cells_all))
    welch_t, fold = lax.map(one_block, jnp.arange(N_GENES, dtype=jnp.int32))
    welch_t = jnp.transpose(welch_t, (1, 0, 2)).reshape(K, G)
    fold = jnp.transpose(fold, (1, 0, 2)).reshape(K, G)
    return (welch_t, fold)
```

```python
import functools

import jax
import jax.numpy as jnp
from jax import lax
from jax.experimental import pallas as pl
from jax.experimental.pallas import tpu as pltpu
from jax.sharding import PartitionSpec as P

MESH = pl.DeviceIdType.MESH
LANES = 128
CHIPS = 4
SLABS = (4, 4, 4, 3)


def welch(sums, squares, total_sum, total_squares, sizes, cells_all):
    mean_in = sums / sizes
    var_in = jnp.maximum((squares - sums * mean_in) / (sizes - 1.0), 0.1)
    rest = cells_all - sizes
    rest_sum = total_sum - sums
    mean_out = rest_sum / rest
    var_out = jnp.maximum((total_squares - squares - rest_sum * mean_out) / (rest - 1.0), 0.1)
    fold = mean_in - mean_out
    return fold / jnp.sqrt(var_in / sizes + var_out / rest), fold


def kernel(slabs, labels_ref, x_ref, t_ref, f_ref, xv, member, lab, row_t, row_f, part, pair, hop, final, *sems):
    (load_sem, pair_send, pair_recv, hop_send, hop_recv, early_send, early_recv, late_send, late_recv,
     lab_send, lab_recv, row_send, row_recv) = sems
    n = len(slabs)
    starts = [sum(slabs[:j]) for j in range(n)]
    clusters, cell_dev = member.shape
    lab_rows = labels_ref.shape[0]
    own = row_t.shape[0]
    genes = row_t.shape[2]
    cells_all = jnp.float32(cell_dev * 2 * CHIPS)

    me = lax.axis_index("cells")
    g = lax.axis_index("genes")
    chip, core = me // 2, me % 2
    right, left, across = (chip + 1) % CHIPS, (chip + 3) % CHIPS, (chip + 2) % CHIPS

    def at_cells(index):
        return {"cells": index, "genes": g}

    def at_genes(index):
        return {"cells": me, "genes": index}

    loads = []
    for j in range(n):
        cols = pl.ds(starts[j] * LANES, slabs[j] * LANES)
        loads.append(pltpu.make_async_copy(x_ref.at[:, cols], xv.at[:, cols], load_sem.at[j]))
        loads[j].start()

    barrier = pltpu.get_barrier_semaphore()
    for d in range(1, 2 * CHIPS):
        pl.semaphore_signal(barrier, inc=1, device_id=at_cells((me + d) % (2 * CHIPS)), device_id_type=MESH)

    @pl.loop(1, own)
    def _(d):
        pl.semaphore_signal(barrier, inc=1, device_id=at_genes((g + d) % own), device_id_type=MESH)

    ids = lax.broadcasted_iota(jnp.int32, (clusters, LANES), 0)
    for r in range(cell_dev // LANES):
        member[:, r * LANES:(r + 1) * LANES] = (ids == labels_ref[r:r + 1, :]).astype(jnp.float32).astype(jnp.bfloat16)

    def rows_of(j):
        return slabs[j] * own

    def compute(j):
        base = starts[j]
        tot = [[], []]
        for s0 in range(0, slabs[j], 2):
            width = min(2, slabs[j] - s0)
            cols = slice((base + s0) * LANES, (base + s0 + width) * LANES)
            x = xv[:, cols]
            wide = x.astype(jnp.float32)
            wide = wide * wide
            high = wide.astype(jnp.bfloat16)
            low = (wide - high.astype(jnp.float32)).astype(jnp.bfloat16)
            m = member[...]
            first = jnp.dot(m, x, preferred_element_type=jnp.float32)
            second = jnp.dot(m, high, preferred_element_type=jnp.float32)
            second += jnp.dot(m, low, preferred_element_type=jnp.float32)
            for kind, res in enumerate((first, second)):
                for w in range(width):
                    piece = res[:, w * LANES:(w + 1) * LANES]
                    s = s0 + w
                    for d in range(2 * CHIPS):
                        part[j][d % 2, d // 2, kind, s * own:(s + 1) * own, :] = piece[d * own:(d + 1) * own, :]
                    tot[kind].append(jnp.sum(piece, axis=0, keepdims=True))
        line = lax.broadcasted_iota(jnp.int32, (8, LANES), 0)
        for kind in range(2):
            block = jnp.zeros((8, LANES), jnp.float32)
            for s in range(slabs[j]):
                block = jnp.where(line == s, tot[kind][s], block)
            for d in range(2 * CHIPS):
                part[j][d % 2, d // 2, kind, rows_of(j):, :] = block

    def remote(src, dst, send, recv, device):
        copy = pltpu.make_async_remote_copy(
            src_ref=src, dst_ref=dst, send_sem=send, recv_sem=recv, device_id=device, device_id_type=MESH
        )
        copy.start()
        return copy

    sent = []

    def share(j):
        copy = remote(part[j].at[1 - core], pair[j], pair_send.at[j], pair_recv.at[j], at_cells(2 * chip + 1 - core))
        sent.append(copy)
        return copy

    def start_x(j, copy):
        copy.wait_recv()
        pair[j][...] += part[j][core]
        copies = []
        for side, to in enumerate((right, left)):
            device = at_cells(2 * to + core)
            copies.append(remote(pair[j].at[across, side], hop[j].at[side], hop_send.at[j, side], hop_recv.at[j, side], device))
            copies.append(remote(pair[j].at[to, 1 - side], final[j].at[side, 1 - side],
                                 early_send.at[j, side], early_recv.at[j, side], device))
        sent.extend(copies)
        return copies

    def forward_x(j, copies):
        out = [copies[1], copies[3]]
        for side, to in enumerate((right, left)):
            copies[2 * side].wait_recv()
            pair[j][to, side] += hop[j][side]
            out.append(remote(pair[j].at[to, side], final[j].at[side, side],
                              late_send.at[j, side], late_recv.at[j, side], at_cells(2 * to + core)))
        sent.extend(out[2:])
        return out

    def finish(j, copies, sizes):
        for copy in copies:
            copy.wait_recv()
        mine = [pair[j][chip, kind] + final[j][0, kind] + final[j][1, kind] for kind in range(2)]
        for s in range(slabs[j]):
            sums, squares = (mine[kind][s * own:(s + 1) * own] for kind in range(2))
            total_sum, total_squares = (mine[kind][rows_of(j) + s:rows_of(j) + s + 1] for kind in range(2))
            t, fold = welch(sums, squares, total_sum, total_squares, sizes, cells_all)
            cols = pl.ds((starts[j] + s) * LANES, LANES)
            row_t[:, :, cols] = t.reshape(own, 1, LANES)
            row_f[:, :, cols] = fold.reshape(own, 1, LANES)
        cols = pl.ds(starts[j] * LANES, slabs[j] * LANES)
        place = pl.ds(pl.multiple_of(g * genes + starts[j] * LANES, LANES), slabs[j] * LANES)

        @pl.loop(1, own)
        def _(d):
            to = (g + d) % own
            for kind, (row, out) in enumerate(((row_t, t_ref), (row_f, f_ref))):
                remote(row.at[to, :, cols], out.at[:, place], row_send.at[kind], row_recv.at[kind], at_genes(to))

        for kind, (row, out) in enumerate(((row_t, t_ref), (row_f, f_ref))):
            pltpu.make_async_copy(row.at[g, :, cols], out.at[:, place], row_recv.at[kind]).start()

    def count():
        for d in range(1, 2 * CHIPS):
            slot = (me + 2 * CHIPS - d) % (2 * CHIPS)
            pltpu.make_async_copy(lab.at[slot], lab.at[slot], lab_recv.at[d]).wait()
        mine = lax.broadcasted_iota(jnp.int32, (own, LANES), 0) + me * own
        counts = jnp.zeros((own, LANES), jnp.float32)
        for d in range(2 * CHIPS):
            for r in range(lab_rows):
                counts += (mine == lab[d, r:r + 1, :]).astype(jnp.float32)
        return jnp.sum(counts, axis=1, keepdims=True)

    pairs, hops, lates = [None] * n, [None] * n, [None] * n
    for j in range(n):
        loads[j].wait()
        compute(j)
        if j == 0:
            pl.semaphore_wait(barrier, 2 * CHIPS - 1 + own - 1)
        pairs[j] = share(j)
        if j == 0:
            for d in range(1, 2 * CHIPS):
                sent.append(remote(labels_ref, lab.at[me], lab_send.at[d], lab_recv.at[d],
                                   at_cells((me + d) % (2 * CHIPS))))
            lab[me] = labels_ref[...]
        if j >= 1:
            hops[j - 1] = start_x(j - 1, pairs[j - 1])
        if j >= 2:
            lates[j - 2] = forward_x(j - 2, hops[j - 2])
    sizes = count()
    hops[n - 1] = start_x(n - 1, pairs[n - 1])
    for j in range(n):
        if lates[j] is None:
            lates[j] = forward_x(j, hops[j])
        if j >= 1:
            finish(j - 1, lates[j - 1], sizes)
    finish(n - 1, lates[n - 1], sizes)

    for copy in sent:
        copy.wait_send()
    for kind, (row, out) in enumerate(((row_t, t_ref), (row_f, f_ref))):
        others = row.at[pl.ds(0, own - 1)]
        pltpu.make_async_copy(others, others, row_send.at[kind]).wait()
        pltpu.make_async_copy(out, out, row_recv.at[kind]).wait()


def on_device(slabs, clusters, expression, labels):
    cell_dev, genes = expression.shape
    own = lax.axis_size("genes")
    n = len(slabs)
    f32 = jnp.float32
    rows = [s * own + 8 for s in slabs]
    dma = pltpu.SemaphoreType.DMA
    line = jax.ShapeDtypeStruct((1, genes * own), f32)
    return pl.pallas_call(
        functools.partial(kernel, slabs),
        out_shape=(line, line),
        in_specs=[pl.BlockSpec(memory_space=pltpu.VMEM), pl.BlockSpec(memory_space=pl.ANY)],
        out_specs=(pl.BlockSpec(memory_space=pl.ANY),) * 2,
        scratch_shapes=[
            pltpu.VMEM((cell_dev, genes), jnp.bfloat16),
            pltpu.VMEM((clusters, cell_dev), jnp.bfloat16),
            pltpu.VMEM((2 * CHIPS, cell_dev // LANES, LANES), jnp.int32),
            pltpu.VMEM((own, 1, genes), f32),
            pltpu.VMEM((own, 1, genes), f32),
            [pltpu.VMEM((2, CHIPS, 2, r, LANES), f32) for r in rows],
            [pltpu.VMEM((CHIPS, 2, r, LANES), f32) for r in rows],
            [pltpu.VMEM((2, r, LANES), f32) for r in rows],
            [pltpu.VMEM((2, 2, r, LANES), f32) for r in rows],
            dma((n,)),
            dma((n,)), dma((n,)),
            dma((n, 2)), dma((n, 2)),
            dma((n, 2)), dma((n, 2)),
            dma((n, 2)), dma((n, 2)),
            dma((2 * CHIPS,)), dma((2 * CHIPS,)),
            dma((2,)), dma((2,)),
        ],
        compiler_params=pltpu.CompilerParams(
            collective_id=0, has_side_effects=True, vmem_limit_bytes=56 * 1024 * 1024
        ),
    )(labels.reshape(cell_dev // LANES, LANES), expression)


def solution(mesh):
    clusters = mesh.shape["cells"] * mesh.shape["genes"]
    return jax.shard_map(
        functools.partial(on_device, SLABS, clusters),
        mesh=mesh,
        in_specs=(P("cells", "genes"), P("cells")),
        out_specs=(P(("cells", "genes"), None), P(("cells", "genes"), None)),
        check_vma=False,
    )
```

```python
import functools

import jax
import jax.numpy as jnp
from jax import lax
from jax.experimental import pallas as pl
from jax.experimental.pallas import tpu as pltpu
from jax.sharding import PartitionSpec as P

MESH = pl.DeviceIdType.MESH
LANES = 128
CHIPS = 4
SLABS = (4, 4, 4, 3)
NY = 4
EXTRA = 16
EAGER, LAG = False, 1
SPAN = 4
ROWS_AFTER = (0, 1, 2, 3)


def kernel(slabs, labels_ref, x_ref, y_ref, xv, member, lab, row, tot_own, tot_pair, tot_chip,
           part, pair, hop, final, load_sem, pair_recv, hop_recv, final_recv, tot_recv, all_recv,
           pair_send, x_send, tot_send, all_send, lab_send, lab_recv, row_send, row_recv):
    n = len(slabs)
    starts = [sum(slabs[:j]) for j in range(n)]
    clusters, cell_dev = member.shape[0] - EXTRA, member.shape[1]
    lab_rows = labels_ref.shape[0]
    own = row.shape[0]
    cells_all = jnp.float32(cell_dev * 2 * CHIPS)

    me = lax.axis_index("cells")
    g = lax.axis_index("genes")
    chip, core = me // 2, me % 2
    right, left, across = (chip + 1) % CHIPS, (chip + 3) % CHIPS, (chip + 2) % CHIPS

    def at_cells(index):
        return {"cells": index, "genes": g}

    def at_genes(index):
        return {"cells": me, "genes": index}

    loads = []
    for j in range(n):
        cols = pl.ds(starts[j] * LANES, slabs[j] * LANES)
        loads.append(pltpu.make_async_copy(x_ref.at[:, cols], xv.at[:, cols], load_sem.at[j]))
        loads[j].start()

    barrier = pltpu.get_barrier_semaphore()
    for d in range(1, 2 * CHIPS):
        pl.semaphore_signal(barrier, inc=1, device_id=at_cells((me + d) % (2 * CHIPS)), device_id_type=MESH)

    peers = {}
    for far in range(own // NY):
        level = lax.rem(lax.div(g, NY) + far, own // NY) * NY
        for d in range(0 if far else 1, NY):
            peers[far, d] = level + lax.rem(g + d, NY)
            pl.semaphore_signal(barrier, inc=1, device_id=at_genes(peers[far, d]), device_id_type=MESH)

    ids = lax.broadcasted_iota(jnp.int32, (clusters, LANES), 0)
    for r in range(cell_dev // LANES):
        hits = (ids == labels_ref[r:r + 1, :]).astype(jnp.float32).astype(jnp.bfloat16)
        member[:clusters, r * LANES:(r + 1) * LANES] = hits
    member[clusters:, :] = jnp.ones((EXTRA, cell_dev), jnp.bfloat16)
    tot_own[...] = jnp.zeros_like(tot_own)

    def rows_of(j):
        return pl.ds(starts[j] * own, slabs[j] * own)

    def compute(j):
        for s0 in range(0, slabs[j], 2):
            width = min(2, slabs[j] - s0)
            base = starts[j] + s0
            x = xv[:, base * LANES:(base + width) * LANES]
            wide = x.astype(jnp.float32)
            wide = wide * wide
            high = wide.astype(jnp.bfloat16)
            low = (wide - high.astype(jnp.float32)).astype(jnp.bfloat16)
            m = member[...]
            first = jnp.dot(m, x, preferred_element_type=jnp.float32)
            second = jnp.dot(m, high, preferred_element_type=jnp.float32)
            second += jnp.dot(m, low, preferred_element_type=jnp.float32)
            for kind, res in enumerate((first, second)):
                for w in range(width):
                    piece = res[:, w * LANES:(w + 1) * LANES]
                    s = base + w
                    for d in range(2 * CHIPS):
                        part[d % 2, d // 2, kind, s * own:(s + 1) * own, :] = piece[d * own:(d + 1) * own, :]
                    span, place = s // SPAN, s % SPAN + SPAN * kind
                    tot_own[span, place:place + 1, :] = piece[clusters:clusters + 1, :]

    def remote(src, dst, send, recv, device):
        pltpu.make_async_remote_copy(
            src_ref=src, dst_ref=dst, send_sem=send, recv_sem=recv, device_id=device, device_id_type=MESH
        ).start()

    def arrived(ref, sem):
        pltpu.make_async_copy(ref, ref, sem).wait()

    spans = {}
    for span in range(tot_own.shape[0]):
        last = min((span + 1) * SPAN, sum(slabs)) - 1
        j = max(j for j in range(n) if starts[j] <= last)
        spans.setdefault(j, []).append(span)

    def share(j):
        partner = at_cells(2 * chip + 1 - core)
        rows = rows_of(j)
        remote(part.at[1 - core, :, :, rows], pair.at[:, :, rows], pair_send, pair_recv.at[j], partner)
        for span in spans.get(j, ()):
            remote(tot_own.at[span], tot_pair.at[span], tot_send, tot_recv.at[span], partner)

    def start_x(j):
        rows = rows_of(j)
        arrived(pair.at[:, :, rows], pair_recv.at[j])
        pair[:, :, rows] += part[core, :, :, rows]
        for side, to in enumerate((right, left)):
            remote(pair.at[across, side, rows], hop.at[side, rows], x_send, hop_recv.at[j], at_cells(2 * to + core))
        for span in spans.get(j, ()):
            arrived(tot_pair.at[span], tot_recv.at[span])
            tot_chip[span, chip] = tot_own[span] + tot_pair[span]
            for d in (2, 1, 3):
                remote(tot_chip.at[span, chip], tot_chip.at[span, chip], all_send, all_recv.at[span],
                       at_cells((me + 2 * d) % (2 * CHIPS)))

    def early_x(j):
        rows = rows_of(j)
        for side, to in enumerate((right, left)):
            remote(pair.at[to, 1 - side, rows], final.at[side, 1 - side, rows], x_send, final_recv.at[j],
                   at_cells(2 * to + core))

    def forward_x(j):
        rows = rows_of(j)
        arrived(hop.at[:, rows], hop_recv.at[j])
        for side, to in enumerate((right, left)):
            pair[to, side, rows] += hop[side, rows]
            remote(pair.at[to, side, rows], final.at[side, side, rows], x_send, final_recv.at[j],
                   at_cells(2 * to + core))

    totals = {}
    rows_from = [0]

    def finish(j):
        rows = rows_of(j)
        arrived(final.at[:, :, rows], final_recv.at[j])
        rest = cells_all - sizes
        per_in, per_in_1, per_out, per_out_1 = 1.0 / sizes, 1.0 / (sizes - 1.0), 1.0 / rest, 1.0 / (rest - 1.0)
        mine = [pair[chip, kind, rows] + final[0, kind, rows] + final[1, kind, rows] for kind in range(2)]
        for s in range(slabs[j]):
            span, place = (starts[j] + s) // SPAN, (starts[j] + s) % SPAN
            if span not in totals:
                arrived(tot_chip.at[span, pl.ds(0, CHIPS - 1)], all_recv.at[span])
                totals[span] = (tot_chip[span, 0] + tot_chip[span, 1]) + (tot_chip[span, 2] + tot_chip[span, 3])
            total_sum = totals[span][place:place + 1]
            total_squares = totals[span][SPAN + place:SPAN + place + 1]
            sums, squares = (mine[kind][s * own:(s + 1) * own] for kind in range(2))
            mean_in = sums * per_in
            var_in = jnp.maximum((squares - sums * mean_in) * per_in_1, 0.1)
            rest_sum = total_sum - sums
            mean_out = rest_sum * per_out
            var_out = jnp.maximum((total_squares - squares - rest_sum * mean_out) * per_out_1, 0.1)
            fold = mean_in - mean_out
            t = fold / jnp.sqrt(var_in * per_in + var_out * per_out)
            cols = pl.ds((starts[j] + s) * LANES, LANES)
            row[:, 0, :, cols] = t.reshape(own, 1, LANES)
            row[:, 1, :, cols] = fold.reshape(own, 1, LANES)
        if j not in ROWS_AFTER:
            return
        end = starts[j] + slabs[j]
        cols = pl.ds(rows_from[0] * LANES, (end - rows_from[0]) * LANES)
        rows_from[0] = end
        for far in sorted(range(own // NY), key=lambda d: -min(d, own // NY - d)):

            for d in range(0 if far else 1, NY):
                to = peers[far, d]
                remote(row.at[to, :, :, cols], y_ref.at[g, :, :, cols], row_send, row_recv, at_genes(to))

        pltpu.make_async_copy(row.at[g, :, :, cols], y_ref.at[g, :, :, cols], row_recv).start()

    def count():
        arrived(lab.at[pl.ds(0, 2 * CHIPS - 1)], lab_recv)
        mine = lax.broadcasted_iota(jnp.int32, (own, LANES), 0) + me * own
        counts = jnp.zeros((own, LANES), jnp.float32)
        for d in range(2 * CHIPS):
            for r in range(lab_rows):
                counts += (mine == lab[d, r:r + 1, :]).astype(jnp.float32)
        return jnp.sum(counts, axis=1, keepdims=True)

    def begin(j):
        loads[j].wait()
        compute(j)
        if j == 0:
            pl.semaphore_wait(barrier, 2 * CHIPS - 1 + own - 1)
        share(j)

    begin(0)
    for d in range(1, 2 * CHIPS):
        remote(labels_ref, lab.at[me], lab_send, lab_recv, at_cells((me + d) % (2 * CHIPS)))
    lab[me] = labels_ref[...]
    begin(1)
    start_x(0)
    early_x(0)
    sizes = None
    for j in range(n):
        if j + 2 < n:
            begin(j + 2)
        if j + 1 < n:
            start_x(j + 1)
        if EAGER and j + 1 < n:
            early_x(j + 1)
        forward_x(j)
        if not EAGER and j + 1 < n:
            early_x(j + 1)
        if sizes is None:
            sizes = count()
        if j >= LAG:
            finish(j - LAG)
    for j in range(n - LAG, n):
        finish(j)

    arrived(part.at[0], pair_send)
    arrived(part.at[0, pl.ds(0, 3)], x_send)
    arrived(tot_own, tot_send)
    arrived(tot_chip.at[:, pl.ds(0, 3)], all_send)
    arrived(lab.at[pl.ds(0, 2 * CHIPS - 1)], lab_send)
    arrived(row.at[pl.ds(0, own - 1)], row_send)
    arrived(y_ref, row_recv)


def split(y_ref, t_ref, f_ref, sem):
    copies = [pltpu.make_async_copy(y_ref.at[:, kind], out, sem.at[kind]) for kind, out in enumerate((t_ref, f_ref))]
    for copy in copies:
        copy.start()
    for copy in copies:
        copy.wait()


def on_device(slabs, clusters, expression, labels):
    cell_dev, genes = expression.shape
    own = lax.axis_size("genes")
    n = len(slabs)
    f32 = jnp.float32
    rows = sum(slabs) * own
    spans = -(-sum(slabs) // SPAN)
    dma = pltpu.SemaphoreType.DMA
    y = pl.pallas_call(
        functools.partial(kernel, slabs),
        out_shape=jax.ShapeDtypeStruct((own, 2, 1, genes), f32),
        in_specs=[pl.BlockSpec(memory_space=pltpu.VMEM), pl.BlockSpec(memory_space=pl.ANY)],
        out_specs=pl.BlockSpec(memory_space=pl.ANY),
        scratch_shapes=[
            pltpu.VMEM((cell_dev, genes), jnp.bfloat16),
            pltpu.VMEM((clusters + EXTRA, cell_dev), jnp.bfloat16),
            pltpu.VMEM((2 * CHIPS, cell_dev // LANES, LANES), jnp.int32),
            pltpu.VMEM((own, 2, 1, genes), f32),
            pltpu.VMEM((spans, 2 * SPAN, LANES), f32),
            pltpu.VMEM((spans, 2 * SPAN, LANES), f32),
            pltpu.VMEM((spans, CHIPS, 2 * SPAN, LANES), f32),
            pltpu.VMEM((2, CHIPS, 2, rows, LANES), f32),
            pltpu.VMEM((CHIPS, 2, rows, LANES), f32),
            pltpu.VMEM((2, rows, LANES), f32),
            pltpu.VMEM((2, 2, rows, LANES), f32),
            dma((n,)), dma((n,)), dma((n,)), dma((n,)), dma((spans,)), dma((spans,)),
            dma, dma, dma, dma, dma, dma, dma, dma,
        ],
        compiler_params=pltpu.CompilerParams(
            collective_id=0, has_side_effects=True, vmem_limit_bytes=56 * 1024 * 1024
        ),
    )(labels.reshape(cell_dev // LANES, LANES), expression)
    line = jax.ShapeDtypeStruct((own, 1, genes), f32)
    t, fold = pl.pallas_call(
        split,
        out_shape=(line, line),
        in_specs=[pl.BlockSpec(memory_space=pltpu.VMEM)],
        out_specs=(pl.BlockSpec(memory_space=pl.ANY),) * 2,
        scratch_shapes=[dma((2,))],
    )(y)
    return t.reshape(1, own * genes), fold.reshape(1, own * genes)


def solution(mesh):
    clusters = mesh.shape["cells"] * mesh.shape["genes"]
    return jax.shard_map(
        functools.partial(on_device, SLABS, clusters),
        mesh=mesh,
        in_specs=(P("cells", "genes"), P("cells")),
        out_specs=(P(("cells", "genes"), None), P(("cells", "genes"), None)),
        check_vma=False,
    )
```

```python
import functools

import jax
import jax.numpy as jnp
from jax import lax
from jax.experimental import pallas as pl
from jax.experimental.pallas import tpu as pltpu
from jax.sharding import PartitionSpec as P

MESH = pl.DeviceIdType.MESH
LANES = 128
CHIPS = 4
SLABS = (4, 4, 3, 2, 2)
NY = 4
PIECES = 4
EXTRA = 16
ORDER = (
    "b0", "b1", "s0", "e0", "b2", "s1", "b3", "e1", "f0", "b4",
    "s2", "f1", "s3", "s4", "e2", "n0", "f2", "e3", "n1", "f3",
    "e4", "f4", "n2", "n3", "n4",
)
SPAN = 4
ROWS_AFTER = (0, 1, 2, 3, 4)


def kernel(slabs, labels_ref, x_ref, y_ref, xv, member, lab, row, tot_own, tot_pair, tot_chip,
           part, pair, hop, final, load_sem, pair_recv, hop_recv, final_recv, tot_recv, all_recv,
           pair_send, x_send, tot_send, all_send, lab_send, lab_recv, row_send, row_recv, label_sem):
    n = len(slabs)
    starts = [sum(slabs[:j]) for j in range(n)]
    clusters, cell_dev = member.shape[0] - EXTRA, member.shape[1]
    lab_rows = lab.shape[1]
    own = row.shape[0]
    cells_all = jnp.float32(cell_dev * 2 * CHIPS)

    me = lax.axis_index("cells")
    g = lax.axis_index("genes")
    chip, core = me // 2, me % 2
    right, left, across = (chip + 1) % CHIPS, (chip + 3) % CHIPS, (chip + 2) % CHIPS

    def at_cells(index):
        return {"cells": index, "genes": g}

    def at_genes(index):
        return {"cells": me, "genes": index}

    own_labels = pltpu.make_async_copy(labels_ref, lab.at[lax.axis_index("cells")], label_sem)
    own_labels.start()
    loads = []
    for j in range(n):
        cols = pl.ds(starts[j] * LANES, slabs[j] * LANES)
        loads.append(pltpu.make_async_copy(x_ref.at[:, cols], xv.at[:, cols], load_sem.at[j]))
        if j == 0:
            loads[j].start()

    barrier = pltpu.get_barrier_semaphore()
    for d in range(1, 2 * CHIPS):
        pl.semaphore_signal(barrier, inc=1, device_id=at_cells((me + d) % (2 * CHIPS)), device_id_type=MESH)

    peers = {}
    for far in range(own // NY):
        level = lax.rem(lax.div(g, NY) + far, own // NY) * NY
        for d in range(0 if far else 1, NY):
            peers[far, d] = level + lax.rem(g + d, NY)
            pl.semaphore_signal(barrier, inc=1, device_id=at_genes(peers[far, d]), device_id_type=MESH)

    ids = lax.broadcasted_iota(jnp.int32, (clusters, LANES), 0)
    own_labels.wait()
    for r in range(cell_dev // LANES):
        hits = (ids == lab[me, r:r + 1, :]).astype(jnp.float32).astype(jnp.bfloat16)
        member[:clusters, r * LANES:(r + 1) * LANES] = hits
    member[clusters:, :] = jnp.ones((EXTRA, cell_dev), jnp.bfloat16)
    tot_own[...] = jnp.zeros_like(tot_own)

    def rows_of(j):
        return pl.ds(starts[j] * own, slabs[j] * own)

    def compute(j):
        for s0 in range(0, slabs[j], 2):
            width = min(2, slabs[j] - s0)
            base = starts[j] + s0
            x = xv[:, base * LANES:(base + width) * LANES]
            wide = x.astype(jnp.float32)
            wide = wide * wide
            high = wide.astype(jnp.bfloat16)
            low = (wide - high.astype(jnp.float32)).astype(jnp.bfloat16)
            m = member[...]
            first = jnp.dot(m, x, preferred_element_type=jnp.float32)
            second = jnp.dot(m, high, preferred_element_type=jnp.float32)
            second += jnp.dot(m, low, preferred_element_type=jnp.float32)
            for kind, res in enumerate((first, second)):
                for w in range(width):
                    piece = res[:, w * LANES:(w + 1) * LANES]
                    s = base + w
                    for d in range(2 * CHIPS):
                        part[d % 2, d // 2, kind, s * own:(s + 1) * own, :] = piece[d * own:(d + 1) * own, :]
                    span, place = s // SPAN, s % SPAN + SPAN * kind
                    tot_own[span, place:place + 1, :] = piece[clusters:clusters + 1, :]

    def remote(src, dst, send, recv, device):
        pltpu.make_async_remote_copy(
            src_ref=src, dst_ref=dst, send_sem=send, recv_sem=recv, device_id=device, device_id_type=MESH
        ).start()

    def arrived(ref, sem):
        pltpu.make_async_copy(ref, ref, sem).wait()

    spans = {}
    for span in range(tot_own.shape[0]):
        last = min((span + 1) * SPAN, sum(slabs)) - 1
        j = max(j for j in range(n) if starts[j] <= last)
        spans.setdefault(j, []).append(span)

    def share(j):
        partner = at_cells(2 * chip + 1 - core)
        rows = rows_of(j)
        remote(part.at[1 - core, :, :, rows], pair.at[:, :, rows], pair_send, pair_recv.at[j], partner)
        for span in spans.get(j, ()):
            remote(tot_own.at[span], tot_pair.at[span], tot_send, tot_recv.at[span], partner)

    def start_x(j):
        rows = rows_of(j)
        arrived(pair.at[:, :, rows], pair_recv.at[j])
        pair[:, :, rows] += part[core, :, :, rows]
        for side, to in enumerate((right, left)):
            remote(pair.at[across, side, rows], hop.at[side, rows], x_send, hop_recv.at[j], at_cells(2 * to + core))
        for span in spans.get(j, ()):
            arrived(tot_pair.at[span], tot_recv.at[span])
            tot_chip[span, chip] = tot_own[span] + tot_pair[span]
            for d in (2, 1, 3):
                remote(tot_chip.at[span, chip], tot_chip.at[span, chip], all_send, all_recv.at[span],
                       at_cells((me + 2 * d) % (2 * CHIPS)))

    def early_x(j):
        rows = rows_of(j)
        for side, to in enumerate((right, left)):
            remote(pair.at[to, 1 - side, rows], final.at[side, 1 - side, rows], x_send, final_recv.at[j],
                   at_cells(2 * to + core))

    def forward_x(j):
        rows = rows_of(j)
        arrived(hop.at[:, rows], hop_recv.at[j])
        for side, to in enumerate((right, left)):
            pair[to, side, rows] += hop[side, rows]
            remote(pair.at[to, side, rows], final.at[side, side, rows], x_send, final_recv.at[j],
                   at_cells(2 * to + core))

    totals = {}
    rows_from = [0]

    def finish(j):
        rows = rows_of(j)
        arrived(final.at[:, :, rows], final_recv.at[j])
        rest = cells_all - sizes
        per_in, per_in_1, per_out, per_out_1 = 1.0 / sizes, 1.0 / (sizes - 1.0), 1.0 / rest, 1.0 / (rest - 1.0)
        mine = [pair[chip, kind, rows] + final[0, kind, rows] + final[1, kind, rows] for kind in range(2)]
        for s in range(slabs[j]):
            span, place = (starts[j] + s) // SPAN, (starts[j] + s) % SPAN
            if span not in totals:
                arrived(tot_chip.at[span, pl.ds(0, CHIPS - 1)], all_recv.at[span])
                totals[span] = (tot_chip[span, 0] + tot_chip[span, 1]) + (tot_chip[span, 2] + tot_chip[span, 3])
            total_sum = totals[span][place:place + 1]
            total_squares = totals[span][SPAN + place:SPAN + place + 1]
            sums, squares = (mine[kind][s * own:(s + 1) * own] for kind in range(2))
            mean_in = sums * per_in
            var_in = jnp.maximum((squares - sums * mean_in) * per_in_1, 0.1)
            rest_sum = total_sum - sums
            mean_out = rest_sum * per_out
            var_out = jnp.maximum((total_squares - squares - rest_sum * mean_out) * per_out_1, 0.1)
            fold = mean_in - mean_out
            t = fold / jnp.sqrt(var_in * per_in + var_out * per_out)
            cols = pl.ds((starts[j] + s) * LANES, LANES)
            row[:, 0, :, cols] = t.reshape(own, 1, LANES)
            row[:, 1, :, cols] = fold.reshape(own, 1, LANES)
        if j not in ROWS_AFTER:
            return
        end = starts[j] + slabs[j]
        cols = pl.ds(rows_from[0] * LANES, (end - rows_from[0]) * LANES)
        rows_from[0] = end
        for far in sorted(range(own // NY), key=lambda d: -min(d, own // NY - d)):

            for d in range(0 if far else 1, NY):
                to = peers[far, d]
                remote(row.at[to, :, :, cols], y_ref.at[g, :, :, cols], row_send, row_recv, at_genes(to))

        pltpu.make_async_copy(row.at[g, :, :, cols], y_ref.at[g, :, :, cols], row_recv).start()

    def count():
        arrived(lab.at[pl.ds(0, 2 * CHIPS - 1)], lab_recv)
        mine = lax.broadcasted_iota(jnp.int32, (own, LANES), 0) + me * own
        counts = jnp.zeros((own, LANES), jnp.float32)
        for d in range(2 * CHIPS):
            for r in range(lab_rows):
                counts += (mine == lab[d, r:r + 1, :]).astype(jnp.float32)
        return jnp.sum(counts, axis=1, keepdims=True)

    def begin(j):
        loads[j].wait()
        if j == 0:
            for load in loads[1:]:
                load.start()
        compute(j)
        if j == 0:
            pl.semaphore_wait(barrier, 2 * CHIPS - 1 + own - 1)
        share(j)
        if j == 0:
            for d in range(1, 2 * CHIPS):
                remote(lab.at[me], lab.at[me], lab_send, lab_recv, at_cells((me + d) % (2 * CHIPS)))

    steps = {"b": begin, "s": start_x, "e": early_x, "f": forward_x, "n": finish}
    sizes = None
    for step in ORDER:
        if step[0] == "n" and sizes is None:
            sizes = count()
        steps[step[0]](int(step[1]))

    arrived(part.at[0], pair_send)
    arrived(part.at[0, pl.ds(0, 3)], x_send)
    arrived(tot_own, tot_send)
    arrived(tot_chip.at[:, pl.ds(0, 3)], all_send)
    arrived(lab.at[pl.ds(0, 2 * CHIPS - 1)], lab_send)
    arrived(row.at[pl.ds(0, own - 1)], row_send)
    arrived(y_ref, row_recv)


def split(y_ref, t_ref, f_ref, held, in_sem, out_sem):
    step = held.shape[0] // PIECES
    pieces = [pl.ds(i * step, step) for i in range(PIECES)]
    loads = [pltpu.make_async_copy(y_ref.at[p], held.at[p], in_sem.at[i]) for i, p in enumerate(pieces)]
    for load in loads:
        load.start()
    stores = []
    for i, p in enumerate(pieces):
        loads[i].wait()
        for kind, out in enumerate((t_ref, f_ref)):
            stores.append(pltpu.make_async_copy(held.at[p, kind], out.at[p], out_sem.at[i, kind]))
            stores[-1].start()
    for store in stores:
        store.wait()


def on_device(slabs, clusters, expression, labels):
    cell_dev, genes = expression.shape
    own = lax.axis_size("genes")
    n = len(slabs)
    f32 = jnp.float32
    rows = sum(slabs) * own
    spans = -(-sum(slabs) // SPAN)
    dma = pltpu.SemaphoreType.DMA
    y = pl.pallas_call(
        functools.partial(kernel, slabs),
        out_shape=jax.ShapeDtypeStruct((own, 2, 1, genes), f32),
        in_specs=[pl.BlockSpec(memory_space=pltpu.HBM), pl.BlockSpec(memory_space=pl.ANY)],
        out_specs=pl.BlockSpec(memory_space=pl.ANY),
        scratch_shapes=[
            pltpu.VMEM((cell_dev, genes), jnp.bfloat16),
            pltpu.VMEM((clusters + EXTRA, cell_dev), jnp.bfloat16),
            pltpu.VMEM((2 * CHIPS, cell_dev // LANES, LANES), jnp.int32),
            pltpu.VMEM((own, 2, 1, genes), f32),
            pltpu.VMEM((spans, 2 * SPAN, LANES), f32),
            pltpu.VMEM((spans, 2 * SPAN, LANES), f32),
            pltpu.VMEM((spans, CHIPS, 2 * SPAN, LANES), f32),
            pltpu.VMEM((2, CHIPS, 2, rows, LANES), f32),
            pltpu.VMEM((CHIPS, 2, rows, LANES), f32),
            pltpu.VMEM((2, rows, LANES), f32),
            pltpu.VMEM((2, 2, rows, LANES), f32),
            dma((n,)), dma((n,)), dma((n,)), dma((n,)), dma((spans,)), dma((spans,)),
            dma, dma, dma, dma, dma, dma, dma, dma, dma,
        ],
        compiler_params=pltpu.CompilerParams(
            collective_id=0, has_side_effects=True, vmem_limit_bytes=56 * 1024 * 1024
        ),
    )(labels.reshape(cell_dev // LANES, LANES), expression)
    line = jax.ShapeDtypeStruct((own, 1, genes), f32)
    t, fold = pl.pallas_call(
        split,
        out_shape=(line, line),
        in_specs=[pl.BlockSpec(memory_space=pltpu.HBM)],
        out_specs=(pl.BlockSpec(memory_space=pl.ANY),) * 2,
        scratch_shapes=[pltpu.VMEM((own, 2, 1, genes), f32), dma((PIECES,)), dma((PIECES, 2))],
    )(y)
    return t.reshape(1, own * genes), fold.reshape(1, own * genes)


def solution(mesh):
    clusters = mesh.shape["cells"] * mesh.shape["genes"]
    return jax.shard_map(
        functools.partial(on_device, SLABS, clusters),
        mesh=mesh,
        in_specs=(P("cells", "genes"), P("cells")),
        out_specs=(P(("cells", "genes"), None), P(("cells", "genes"), None)),
        check_vma=False,
    )
```

```python
import functools

import jax
import jax.numpy as jnp
from jax import lax
from jax.experimental import pallas as pl
from jax.experimental.pallas import tpu as pltpu
from jax.sharding import PartitionSpec as P

MESH = pl.DeviceIdType.MESH
LANES = 128
CHIPS = 4
SLABS = (4, 4, 3, 2, 2)
NY = 4
PIECES = 4
EXTRA = 16
ORDER = (
    "b0", "c0", "b1", "s0", "e0", "c1", "b2", "c2", "s1", "b3", "e1", "f0", "b4",
    "s2", "f1", "s3", "s4", "e2", "n0", "f2", "e3", "n1", "f3",
    "e4", "f4", "n2", "n3", "n4",
)
SPAN = 4
ROWS_AFTER = (0, 1, 2, 3, 4)


def kernel(slabs, labels_ref, x_ref, y_ref, xv, member, lab, row, tot_own, tot_pair, tot_chip,
           part, pair, hop, final, load_sem, pair_recv, hop_recv, final_recv, tot_recv, all_recv,
           pair_send, x_send, tot_send, all_send, lab_send, lab_recv, row_send, row_recv, label_sem):
    n = len(slabs)
    starts = [sum(slabs[:j]) for j in range(n)]
    clusters, cell_dev = member.shape[0] - EXTRA, member.shape[1]
    lab_rows = lab.shape[1]
    own = row.shape[0]
    cells_all = jnp.float32(cell_dev * 2 * CHIPS)

    me = lax.axis_index("cells")
    g = lax.axis_index("genes")
    chip, core = me // 2, me % 2
    right, left, across = (chip + 1) % CHIPS, (chip + 3) % CHIPS, (chip + 2) % CHIPS

    def at_cells(index):
        return {"cells": index, "genes": g}

    def at_genes(index):
        return {"cells": me, "genes": index}

    own_labels = pltpu.make_async_copy(labels_ref, lab.at[lax.axis_index("cells")], label_sem)
    own_labels.start()
    loads = []
    for j in range(n):
        cols = pl.ds(starts[j] * LANES, slabs[j] * LANES)
        loads.append(pltpu.make_async_copy(x_ref.at[:, cols], xv.at[:, cols], load_sem.at[j]))
        if j == 0:
            loads[j].start()

    barrier = pltpu.get_barrier_semaphore()
    for d in range(1, 2 * CHIPS):
        pl.semaphore_signal(barrier, inc=1, device_id=at_cells((me + d) % (2 * CHIPS)), device_id_type=MESH)

    peers = {}
    for far in range(own // NY):
        level = lax.rem(lax.div(g, NY) + far, own // NY) * NY
        for d in range(0 if far else 1, NY):
            peers[far, d] = level + lax.rem(g + d, NY)
            pl.semaphore_signal(barrier, inc=1, device_id=at_genes(peers[far, d]), device_id_type=MESH)

    ids = lax.broadcasted_iota(jnp.int32, (clusters, LANES), 0)
    own_labels.wait()
    for r in range(cell_dev // LANES):
        hits = (ids == lab[me, r:r + 1, :]).astype(jnp.float32).astype(jnp.bfloat16)
        member[:clusters, r * LANES:(r + 1) * LANES] = hits
    member[clusters:, :] = jnp.ones((EXTRA, cell_dev), jnp.bfloat16)
    tot_own[...] = jnp.zeros_like(tot_own)

    def rows_of(j):
        return pl.ds(starts[j] * own, slabs[j] * own)

    def compute(j, blocks):
        for s0 in blocks:
            width = min(2, slabs[j] - s0)
            base = starts[j] + s0
            x = xv[:, base * LANES:(base + width) * LANES]
            wide = x.astype(jnp.float32)
            wide = wide * wide
            high = wide.astype(jnp.bfloat16)
            low = (wide - high.astype(jnp.float32)).astype(jnp.bfloat16)
            m = member[...]
            first = jnp.dot(m, x, preferred_element_type=jnp.float32)
            second = jnp.dot(m, high, preferred_element_type=jnp.float32)
            second += jnp.dot(m, low, preferred_element_type=jnp.float32)
            for kind, res in enumerate((first, second)):
                for w in range(width):
                    piece = res[:, w * LANES:(w + 1) * LANES]
                    s = base + w
                    for d in range(2 * CHIPS):
                        part[d % 2, d // 2, kind, s * own:(s + 1) * own, :] = piece[d * own:(d + 1) * own, :]
                    span, place = s // SPAN, s % SPAN + SPAN * kind
                    tot_own[span, place:place + 1, :] = piece[clusters:clusters + 1, :]

    def remote(src, dst, send, recv, device):
        pltpu.make_async_remote_copy(
            src_ref=src, dst_ref=dst, send_sem=send, recv_sem=recv, device_id=device, device_id_type=MESH
        ).start()

    def arrived(ref, sem):
        pltpu.make_async_copy(ref, ref, sem).wait()

    spans = {}
    for span in range(tot_own.shape[0]):
        last = min((span + 1) * SPAN, sum(slabs)) - 1
        j = max(j for j in range(n) if starts[j] <= last)
        spans.setdefault(j, []).append(span)

    def share(j, first, last):
        partner = at_cells(2 * chip + 1 - core)
        rows = pl.ds((starts[j] + first) * own, (last - first) * own)
        remote(part.at[1 - core, :, :, rows], pair.at[:, :, rows], pair_send, pair_recv.at[j], partner)
        for span in spans.get(j, ()) if last == slabs[j] else ():
            remote(tot_own.at[span], tot_pair.at[span], tot_send, tot_recv.at[span], partner)

    def start_x(j):
        rows = rows_of(j)
        arrived(pair.at[:, :, rows], pair_recv.at[j])
        pair[:, :, rows] += part[core, :, :, rows]
        for side, to in enumerate((right, left)):
            remote(pair.at[across, side, rows], hop.at[side, rows], x_send, hop_recv.at[j], at_cells(2 * to + core))
        for span in spans.get(j, ()):
            arrived(tot_pair.at[span], tot_recv.at[span])
            tot_chip[span, chip] = tot_own[span] + tot_pair[span]
            for d in (2, 1, 3):
                remote(tot_chip.at[span, chip], tot_chip.at[span, chip], all_send, all_recv.at[span],
                       at_cells((me + 2 * d) % (2 * CHIPS)))

    def early_x(j):
        rows = rows_of(j)
        for side, to in enumerate((right, left)):
            remote(pair.at[to, 1 - side, rows], final.at[side, 1 - side, rows], x_send, final_recv.at[j],
                   at_cells(2 * to + core))

    def forward_x(j):
        rows = rows_of(j)
        arrived(hop.at[:, rows], hop_recv.at[j])
        for side, to in enumerate((right, left)):
            pair[to, side, rows] += hop[side, rows]
            remote(pair.at[to, side, rows], final.at[side, side, rows], x_send, final_recv.at[j],
                   at_cells(2 * to + core))

    totals = {}
    rows_from = [0]

    def finish(j):
        rows = rows_of(j)
        arrived(final.at[:, :, rows], final_recv.at[j])
        rest = cells_all - sizes
        per_in, per_in_1, per_out, per_out_1 = 1.0 / sizes, 1.0 / (sizes - 1.0), 1.0 / rest, 1.0 / (rest - 1.0)
        mine = [pair[chip, kind, rows] + final[0, kind, rows] + final[1, kind, rows] for kind in range(2)]
        for s in range(slabs[j]):
            span, place = (starts[j] + s) // SPAN, (starts[j] + s) % SPAN
            if span not in totals:
                arrived(tot_chip.at[span, pl.ds(0, CHIPS - 1)], all_recv.at[span])
                totals[span] = (tot_chip[span, 0] + tot_chip[span, 1]) + (tot_chip[span, 2] + tot_chip[span, 3])
            total_sum = totals[span][place:place + 1]
            total_squares = totals[span][SPAN + place:SPAN + place + 1]
            sums, squares = (mine[kind][s * own:(s + 1) * own] for kind in range(2))
            mean_in = sums * per_in
            var_in = jnp.maximum((squares - sums * mean_in) * per_in_1, 0.1)
            rest_sum = total_sum - sums
            mean_out = rest_sum * per_out
            var_out = jnp.maximum((total_squares - squares - rest_sum * mean_out) * per_out_1, 0.1)
            fold = mean_in - mean_out
            t = fold / jnp.sqrt(var_in * per_in + var_out * per_out)
            cols = pl.ds((starts[j] + s) * LANES, LANES)
            row[:, 0, :, cols] = t.reshape(own, 1, LANES)
            row[:, 1, :, cols] = fold.reshape(own, 1, LANES)
        if j not in ROWS_AFTER:
            return
        end = starts[j] + slabs[j]
        cols = pl.ds(rows_from[0] * LANES, (end - rows_from[0]) * LANES)
        rows_from[0] = end
        for far in sorted(range(own // NY), key=lambda d: -min(d, own // NY - d)):

            for d in range(0 if far else 1, NY):
                to = peers[far, d]
                remote(row.at[to, :, :, cols], y_ref.at[g, :, :, cols], row_send, row_recv, at_genes(to))

        pltpu.make_async_copy(row.at[g, :, :, cols], y_ref.at[g, :, :, cols], row_recv).start()

    def count():
        arrived(lab.at[pl.ds(0, 2 * CHIPS - 1)], lab_recv)
        mine = lax.broadcasted_iota(jnp.int32, (own, LANES), 0) + me * own
        counts = jnp.zeros((own, LANES), jnp.float32)
        for d in range(2 * CHIPS):
            for r in range(lab_rows):
                counts += (mine == lab[d, r:r + 1, :]).astype(jnp.float32)
        return jnp.sum(counts, axis=1, keepdims=True)

    def begin(j):
        loads[j].wait()
        if j == 0:
            for load in loads[1:]:
                load.start()
        compute(j, (0,))
        if j == 0:
            pl.semaphore_wait(barrier, 2 * CHIPS - 1 + own - 1)
        share(j, 0, min(2, slabs[j]))
        if j == 0:
            for d in range(1, 2 * CHIPS):
                remote(lab.at[me], lab.at[me], lab_send, lab_recv, at_cells((me + d) % (2 * CHIPS)))

    def rest(j):
        compute(j, range(2, slabs[j], 2))
        share(j, 2, slabs[j])

    steps = {"b": begin, "c": rest, "s": start_x, "e": early_x, "f": forward_x, "n": finish}
    sizes = None
    for step in ORDER:
        if step[0] == "n" and sizes is None:
            sizes = count()
        steps[step[0]](int(step[1]))

    arrived(part.at[0], pair_send)
    arrived(part.at[0, pl.ds(0, 3)], x_send)
    arrived(tot_own, tot_send)
    arrived(tot_chip.at[:, pl.ds(0, 3)], all_send)
    arrived(lab.at[pl.ds(0, 2 * CHIPS - 1)], lab_send)
    arrived(row.at[pl.ds(0, own - 1)], row_send)
    arrived(y_ref, row_recv)


def split(y_ref, t_ref, f_ref, held, in_sem, out_sem):
    step = held.shape[0] // PIECES
    pieces = [pl.ds(i * step, step) for i in range(PIECES)]
    loads = [pltpu.make_async_copy(y_ref.at[p], held.at[p], in_sem.at[i]) for i, p in enumerate(pieces)]
    for load in loads:
        load.start()
    stores = []
    for i, p in enumerate(pieces):
        loads[i].wait()
        for kind, out in enumerate((t_ref, f_ref)):
            stores.append(pltpu.make_async_copy(held.at[p, kind], out.at[p], out_sem.at[i, kind]))
            stores[-1].start()
    for store in stores:
        store.wait()


def on_device(slabs, clusters, expression, labels):
    cell_dev, genes = expression.shape
    own = lax.axis_size("genes")
    n = len(slabs)
    f32 = jnp.float32
    rows = sum(slabs) * own
    spans = -(-sum(slabs) // SPAN)
    dma = pltpu.SemaphoreType.DMA
    y = pl.pallas_call(
        functools.partial(kernel, slabs),
        out_shape=jax.ShapeDtypeStruct((own, 2, 1, genes), f32),
        in_specs=[pl.BlockSpec(memory_space=pltpu.HBM), pl.BlockSpec(memory_space=pl.ANY)],
        out_specs=pl.BlockSpec(memory_space=pl.ANY),
        scratch_shapes=[
            pltpu.VMEM((cell_dev, genes), jnp.bfloat16),
            pltpu.VMEM((clusters + EXTRA, cell_dev), jnp.bfloat16),
            pltpu.VMEM((2 * CHIPS, cell_dev // LANES, LANES), jnp.int32),
            pltpu.VMEM((own, 2, 1, genes), f32),
            pltpu.VMEM((spans, 2 * SPAN, LANES), f32),
            pltpu.VMEM((spans, 2 * SPAN, LANES), f32),
            pltpu.VMEM((spans, CHIPS, 2 * SPAN, LANES), f32),
            pltpu.VMEM((2, CHIPS, 2, rows, LANES), f32),
            pltpu.VMEM((CHIPS, 2, rows, LANES), f32),
            pltpu.VMEM((2, rows, LANES), f32),
            pltpu.VMEM((2, 2, rows, LANES), f32),
            dma((n,)), dma((n,)), dma((n,)), dma((n,)), dma((spans,)), dma((spans,)),
            dma, dma, dma, dma, dma, dma, dma, dma, dma,
        ],
        compiler_params=pltpu.CompilerParams(
            collective_id=0, has_side_effects=True, vmem_limit_bytes=56 * 1024 * 1024
        ),
    )(labels.reshape(cell_dev // LANES, LANES), expression)
    line = jax.ShapeDtypeStruct((own, 1, genes), f32)
    t, fold = pl.pallas_call(
        split,
        out_shape=(line, line),
        in_specs=[pl.BlockSpec(memory_space=pltpu.HBM)],
        out_specs=(pl.BlockSpec(memory_space=pl.ANY),) * 2,
        scratch_shapes=[pltpu.VMEM((own, 2, 1, genes), f32), dma((PIECES,)), dma((PIECES, 2))],
    )(y)
    return t.reshape(1, own * genes), fold.reshape(1, own * genes)


def solution(mesh):
    clusters = mesh.shape["cells"] * mesh.shape["genes"]
    return jax.shard_map(
        functools.partial(on_device, SLABS, clusters),
        mesh=mesh,
        in_specs=(P("cells", "genes"), P("cells")),
        out_specs=(P(("cells", "genes"), None), P(("cells", "genes"), None)),
        check_vma=False,
    )
```
